32 devices in a mesh: groups: 2 (over y), ctx: 4 (over x, core), head: 4 (over z).
Axes of the slice: x: 2, y: 2, z: 4, core: 2. Of those that a mesh axis runs over, the one named last changes fastest.
Arguments:
- tokens_in: bfloat16 [8192, 4096], P(('groups', 'ctx')), parts along dimension 0, may hold values from -16 to 16
- tempo_ids: int32 [8192], P(('groups', 'ctx')), parts along dimension 0, may hold values from 0 to 63
- tempo_table: bfloat16 [64, 4096], replicated, may hold values from -6 to 6
- w_query: bfloat16 [4096, 2048], P('ctx', 'head'), may hold values from -0.1875 to 0.1875
- w_key: bfloat16 [4096, 2048], P('ctx', 'head'), may hold values from -0.09375 to 0.09375
- w_value: bfloat16 [4096, 2048], P('ctx', 'head'), may hold values from -0.09375 to 0.09375
Outputs:
- attended: bfloat16 [8192, 2048], P(('groups', 'ctx'), 'head'), parts along dimension 0
The draws below stay inside these ranges and needn't reach their ends.
There are 2 independent parts, one for each index of `groups`. The reference program is written for one: setup_inputs(seed, part) draws one part's arguments, and reference() takes and returns one part's arrays. A program takes and returns all parts, laid end to end along the dimension named above; an argument that names none is the same for every part. Nothing has to cross between parts.
All inputs are finite; a program needn't handle non-finite values.
Results may differ from the reference program's by a relative error of at most 0.029.
Values may be sent and summed in bfloat16 or wider, within the bound.
A program may use at most 64 MiB of HBM per device.

```python
import jax
import jax.numpy as jnp
from jax import lax

D = 4096
HEAD_DIM = 128
HEADS = 16
TEMPOS = 64
SPAN = 1024
BEACONS = 32
POOL = 32
TOKENS = 4096


def draw_tokens_in(key, part):
    first = jax.random.fold_in(key, 0)
    base = jnp.clip(jax.random.normal(first, (TOKENS, D), jnp.float32), -6.0, 6.0)
    return base.astype(jnp.bfloat16)


def touch_ends(result, stream_key, low, high):
    spot = [jax.random.randint(jax.random.fold_in(stream_key, axis), (), 0, length) for axis, length in enumerate(result.shape)]
    main_axis = result.shape.index(max(result.shape))
    neighbour = spot[:main_axis] + [(spot[main_axis] + 1) % result.shape[main_axis]] + spot[main_axis + 1:]
    return result.at[tuple(spot)].set(low).at[tuple(neighbour)].set(high)


def block_levels(key, shape, pieces, least, top_value):
    loudness = 1.0
    for dim, shards_of in pieces:
        draws = jax.random.uniform(jax.random.fold_in(jax.random.fold_in(key, 6), dim), (shards_of,), jnp.float32, least / len(pieces), top_value / len(pieces))
        loudness = loudness * jnp.repeat(jnp.exp(draws), shape[dim] // shards_of).reshape((-1,) + (1,) * (len(shape) - 1 - dim))
    return loudness


def bell_draw(own_key, extent, spread, reach, cuts=(), held_as=jnp.bfloat16):
    result = spread * jax.random.normal(own_key, extent, jnp.float32)
    if cuts:
        result = result * block_levels(own_key, extent, cuts, -0.22, 0.18)
    return jnp.clip(result, -reach, reach).astype(held_as)


def setup_inputs(seed: int = 0, part: int = 0) -> dict:
    arg_keys = jax.random.split(jax.random.key(seed), 7)
    part_splits = jax.random.split(jax.random.fold_in(arg_keys[6], part), 7)
    return {
        "tokens_in": draw_tokens_in(jax.random.fold_in(jax.random.fold_in(arg_keys[6], part), 71), part),
        "tempo_ids": touch_ends(jax.random.randint(part_splits[1], (TOKENS,), 0, TEMPOS), jax.random.fold_in(part_splits[1], 1), 0, TEMPOS - 1).astype(jnp.int32),
        "tempo_table": bell_draw(arg_keys[2], (TEMPOS, D), 1.0, 6.0),
        "w_query": bell_draw(arg_keys[3], (D, HEADS * HEAD_DIM), (D // 4) ** -0.5, 0.1875, ((0, 4), (1, 4))),
        "w_key": bell_draw(arg_keys[4], (D, HEADS * HEAD_DIM), D ** -0.5, 0.09375, ((0, 4), (1, 4))),
        "w_value": bell_draw(arg_keys[5], (D, HEADS * HEAD_DIM), D ** -0.5, 0.09375, ((0, 4), (1, 4))),
    }


LOWEST = -1.0e30


def reference(tokens_in, tempo_ids, tempo_table, w_query, w_key, w_value):
    width_all = HEADS * HEAD_DIM
    selector = (tempo_ids[:, None] == jnp.arange(TEMPOS, dtype=jnp.int32)[None, :]).astype(tempo_table.dtype)
    hidden = (tokens_in.astype(jnp.float32) + jnp.dot(selector, tempo_table, preferred_element_type=jnp.float32)).astype(jnp.bfloat16)
    queries = jnp.dot(hidden, w_query, preferred_element_type=jnp.float32).astype(jnp.bfloat16)
    keys = jnp.dot(hidden, w_key, preferred_element_type=jnp.float32).astype(jnp.bfloat16)
    values = jnp.dot(hidden, w_value, preferred_element_type=jnp.float32).astype(jnp.bfloat16)
    span_count = TOKENS // SPAN
    slot_count = span_count * BEACONS
    beacon_keys = (jnp.sum(keys.reshape(slot_count, POOL, width_all).astype(jnp.float32), axis=1) * POOL ** -0.5).astype(jnp.bfloat16)
    beacon_values = (jnp.sum(values.reshape(slot_count, POOL, width_all).astype(jnp.float32), axis=1) * POOL ** -0.5).astype(jnp.bfloat16)
    slot_span = jnp.arange(slot_count, dtype=jnp.int32) // BEACONS
    causal = jnp.arange(SPAN, dtype=jnp.int32)[:, None] >= jnp.arange(SPAN, dtype=jnp.int32)[None, :]

    def one_span(index):
        start = index * SPAN
        span_queries = lax.dynamic_slice_in_dim(queries, start, SPAN, 0).reshape(SPAN, HEADS, HEAD_DIM).astype(jnp.float32)
        span_keys = lax.dynamic_slice_in_dim(keys, start, SPAN, 0).reshape(SPAN, HEADS, HEAD_DIM)
        span_values = lax.dynamic_slice_in_dim(values, start, SPAN, 0).reshape(SPAN, HEADS, HEAD_DIM)
        all_keys = jnp.concatenate([beacon_keys.reshape(slot_count, HEADS, HEAD_DIM), span_keys], axis=0).astype(jnp.float32)
        all_values = jnp.concatenate([beacon_values.reshape(slot_count, HEADS, HEAD_DIM), span_values], axis=0).astype(jnp.float32)
        earlier = jnp.broadcast_to((slot_span < index)[None, :], (SPAN, slot_count))
        allowed = jnp.concatenate([earlier, causal], axis=1)[None]
        scores = jnp.einsum("qhd,khd->hqk", span_queries, all_keys) * (HEAD_DIM ** -0.5)
        masked = jnp.where(allowed, scores, LOWEST)
        highest = jnp.max(masked, axis=2, keepdims=True)
        weights = jnp.where(allowed, jnp.exp(masked - highest), 0.0)
        totals = jnp.sum(weights, axis=2)
        rounded = lax.optimization_barrier(weights.astype(jnp.bfloat16))
        summed = jnp.einsum("hqk,khd->qhd", rounded.astype(jnp.float32), all_values)
        return (summed / totals.T[:, :, None]).reshape(SPAN, width_all).astype(jnp.bfloat16)

    outputs = lax.map(one_span, jnp.arange(span_count, dtype=jnp.int32))
    return outputs.reshape(TOKENS, width_all)
```

```python
import functools
import math

import jax
import jax.numpy as jnp
from jax import lax
from jax.experimental import pallas as pl
from jax.experimental.pallas import tpu as pltpu
from jax.sharding import PartitionSpec as P

HEAD_DIM = 128
SPAN = 1024
BEACONS = 32
POOL = 32


LOWEST = -1e30


def by_heads(matrix, heads_local):
    return matrix.reshape(matrix.shape[0], heads_local, -1).transpose(1, 0, 2)


def partial_attend(queries, keys, values, allowed):
    scores = jnp.einsum(
        "hqd,hkd->hqk", queries, keys, preferred_element_type=jnp.float32
    ) * queries.shape[-1] ** (-0.5)
    masked = jnp.where(allowed, scores, LOWEST)
    highest = jnp.max(masked, axis=2)
    weights = jnp.where(allowed, jnp.exp(masked - highest[..., None]), 0.0)
    totals = jnp.sum(weights, axis=2)
    summed = jnp.einsum(
        "hqk,hkd->hqd", weights.astype(jnp.bfloat16), values, preferred_element_type=jnp.float32
    )
    return (highest, totals, summed)


def combine_partials(first, second):
    highest = jnp.maximum(first[0], second[0])
    left_factor = jnp.exp(first[0] - highest)
    right_factor = jnp.exp(second[0] - highest)
    totals = first[1] * left_factor + second[1] * right_factor
    summed = first[2] * left_factor[..., None] + second[2] * right_factor[..., None]
    return (highest, totals, summed)


def beacon_partial(
    queries, query_span, beacon_keys, beacon_values, low_rank, high_rank, group, slots_dev
):
    heads_local, query_count, head_size = queries.shape
    block_width = group * slots_dev
    start_state = (
        jnp.full((heads_local, query_count), LOWEST, jnp.float32),
        jnp.zeros((heads_local, query_count), jnp.float32),
        jnp.zeros((heads_local, query_count, head_size), jnp.float32),
    )

    def visit(block, state):
        first_slot = block * block_width
        block_keys = lax.dynamic_slice_in_dim(beacon_keys, first_slot, block_width, 1)
        block_values = lax.dynamic_slice_in_dim(beacon_values, first_slot, block_width, 1)
        slot_index = first_slot + jnp.arange(block_width, dtype=jnp.int32)
        owner = slot_index // slots_dev
        in_range = (owner >= low_rank) & (owner < high_rank)
        earlier = (slot_index // BEACONS)[None, :] < query_span[:, None]
        allowed = (in_range[None, :] & earlier)[None]
        return combine_partials(state, partial_attend(queries, block_keys, block_values, allowed))

    first_block = low_rank // group
    last_block = (high_rank + group - 1) // group
    return lax.fori_loop(first_block, last_block, visit, start_state)


def on_device(tokens_in, tempo_ids, tempo_table, w_query, w_key, w_value):
    row_count = tokens_in.shape[0]
    col_width = w_query.shape[1]
    heads_local = col_width // HEAD_DIM
    ctx_count = lax.axis_size("ctx")
    ctx_rank = lax.axis_index("ctx")
    spans_dev = row_count // SPAN
    slots_dev = spans_dev * BEACONS
    target = max(1, 256 // slots_dev)
    group = min(ctx_count, 1 << target.bit_length() - 1)
    selector = (
        tempo_ids[:, None] == jnp.arange(tempo_table.shape[0], dtype=jnp.int32)[None, :]
    ).astype(jnp.bfloat16)
    hidden = (
        tokens_in.astype(jnp.float32)
        + jnp.dot(selector, tempo_table, preferred_element_type=jnp.float32)
    ).astype(jnp.bfloat16)
    pieces = (
        lax.all_gather(w_query, "ctx", axis=0, tiled=True),
        lax.all_gather(w_key, "ctx", axis=0, tiled=True),
        lax.all_gather(w_value, "ctx", axis=0, tiled=True),
    )
    projected = tuple(
        (jnp.dot(hidden, piece, preferred_element_type=jnp.float32) for piece in pieces)
    )
    queries = projected[0].astype(jnp.bfloat16)
    keys = projected[1].astype(jnp.bfloat16)
    values = projected[2].astype(jnp.bfloat16)
    pool_scale = POOL ** (-0.5)
    own_keys = (
        jnp.sum(keys.reshape(slots_dev, POOL, col_width).astype(jnp.float32), axis=1) * pool_scale
    ).astype(jnp.bfloat16)
    own_values = (
        jnp.sum(values.reshape(slots_dev, POOL, col_width).astype(jnp.float32), axis=1) * pool_scale
    ).astype(jnp.bfloat16)
    every_keys, every_values = (
        lax.all_gather(own_keys, "ctx", axis=0, tiled=True),
        lax.all_gather(own_values, "ctx", axis=0, tiled=True),
    )
    beacon_keys = by_heads(every_keys, heads_local)
    beacon_values = by_heads(every_values, heads_local)
    query_heads = by_heads(queries, heads_local)
    local_span = jnp.arange(row_count, dtype=jnp.int32) // SPAN
    own_span = ctx_rank * spans_dev + local_span

    def fold_spans(matrix):
        return by_heads(matrix, heads_local)

    causal = (
        jnp.arange(SPAN, dtype=jnp.int32)[:, None] >= jnp.arange(SPAN, dtype=jnp.int32)[None, :]
    )[None]
    inside = partial_attend(fold_spans(queries), fold_spans(keys), fold_spans(values), causal)
    inside = (inside[0], inside[1], inside[2])
    upper_rank = ctx_rank + 1
    remote = beacon_partial(
        query_heads,
        own_span,
        beacon_keys,
        beacon_values,
        jnp.zeros((), jnp.int32),
        upper_rank,
        group,
        slots_dev,
    )
    highest, totals, summed = combine_partials(inside, remote)
    attended = summed / totals[..., None]
    return attended.transpose(1, 0, 2).reshape(row_count, col_width).astype(jnp.bfloat16)


CHUNK = HEAD_DIM
PAIR = 2 * HEAD_DIM
AHEAD = 3
MESH = pl.DeviceIdType.MESH
QUERY, KEY, VALUE = 0, 1, 2


def song_kernel(
    tokens_hbm,
    ids_ref,
    table_ref,
    wq_hbm,
    wk_hbm,
    wv_hbm,
    out_ref,
    hidden,
    weights,
    partial,
    rounded,
    selector,
    beacons,
    token_sem,
    own_sem,
    x_send,
    x_recv,
    y_send,
    y_recv,
    own_send,
    own_recv,
    cx_send,
    cx_recv,
    cy_send,
    cy_recv,
    b_send,
    b_recv,
):
    rows, depth = hidden.shape
    shard, width = wq_hbm.shape
    pairs = width // PAIR
    half = shard // 2
    near = 2 * shard
    sources = (wq_hbm, wk_hbm, wv_hbm)

    song = lax.axis_index("groups")
    rank = lax.axis_index("ctx")
    chip, core = rank // 2, rank % 2
    far_chip = 1 - chip
    sibling = {"ctx": chip * 2 + 1 - core}
    across = {"ctx": far_chip * 2 + core}
    diagonal = {"ctx": far_chip * 2 + 1 - core}
    twin = {"groups": 1 - song}

    near_row = pl.multiple_of(chip * near, near)
    far_row = pl.multiple_of(far_chip * near, near)
    units = [(kind, pair) for pair in range(pairs) for kind in (KEY, VALUE, QUERY)]
    chunks = [(kind, pair * 2 + side) for kind, pair in units for side in range(2)]
    count = len(chunks)

    def spot(index, owner_chip, owner_core, part):
        kind, block = chunks[index]
        row = pl.multiple_of((owner_chip * 2 + owner_core) * shard + part * half, half)
        return weights.at[kind, pl.ds(row, half), pl.ds(block * CHUNK, CHUNK)]

    def x_copy(index):
        kind, block = chunks[index]
        begin = pl.multiple_of(song * half, half)
        return pltpu.make_async_remote_copy(
            src_ref=sources[kind].at[pl.ds(begin, half), pl.ds(block * CHUNK, CHUNK)],
            dst_ref=spot(index, chip, core, song),
            send_sem=x_send.at[index],
            recv_sem=x_recv.at[index],
            device_id=across,
            device_id_type=MESH,
        )

    def y_copy(index):
        place = spot(index, far_chip, core, song)
        return pltpu.make_async_remote_copy(
            src_ref=place,
            dst_ref=place,
            send_sem=y_send.at[index],
            recv_sem=y_recv.at[index],
            device_id=twin,
            device_id_type=MESH,
        )

    def core_copy(index, part, send, recv):
        place = spot(index, far_chip, core, part)
        return pltpu.make_async_remote_copy(
            src_ref=place,
            dst_ref=place,
            send_sem=send.at[index],
            recv_sem=recv.at[index],
            device_id=sibling,
            device_id_type=MESH,
        )

    def cx_copy(index):
        return core_copy(index, song, cx_send, cx_recv)

    def cy_copy(index):
        return core_copy(index, 1 - song, cy_send, cy_recv)

    def own_place(unit):
        kind, pair = units[unit]
        row = pl.multiple_of(rank * shard, shard)
        return weights.at[kind, pl.ds(row, shard), pl.ds(pair * PAIR, PAIR)]

    def own_source(unit):
        kind, pair = units[unit]
        return sources[kind].at[:, pl.ds(pair * PAIR, PAIR)]

    def own_copy(unit):
        return pltpu.make_async_copy(own_source(unit), own_place(unit), own_sem.at[unit])

    def own_remote(unit):
        return pltpu.make_async_remote_copy(
            src_ref=own_source(unit),
            dst_ref=own_place(unit),
            send_sem=own_send.at[unit],
            recv_sem=own_recv.at[unit],
            device_id=sibling,
            device_id_type=MESH,
        )

    token_step = depth // 4

    def token_copy(block):
        row = near_row if block < 2 else far_row
        start = pl.multiple_of(row + (block % 2) * token_step, token_step)
        place = pl.ds(start, token_step)
        return pltpu.make_async_copy(
            tokens_hbm.at[:, place], hidden.at[:, place], token_sem.at[block]
        )

    def beacon_copies(kind, pair):
        place = beacons.at[kind - 1, pair, pl.ds(pl.multiple_of(rank * BEACONS, BEACONS), BEACONS)]
        result = []
        for number, target in enumerate((sibling, across, diagonal)):
            result.append(
                pltpu.make_async_remote_copy(
                    src_ref=place,
                    dst_ref=place,
                    send_sem=b_send.at[kind - 1, pair, number],
                    recv_sem=b_recv.at[kind - 1, pair, number],
                    device_id=target,
                    device_id_type=MESH,
                )
            )
        return result

    token_copy(0).start()
    token_copy(1).start()
    barrier = pltpu.get_barrier_semaphore()
    partners = (sibling, across, diagonal, twin)
    for target in partners:
        pl.semaphore_signal(barrier, inc=1, device_id=target, device_id_type=MESH)
    pl.semaphore_wait(barrier, len(partners))

    for index in range(AHEAD):
        x_copy(index).start()
    for unit in range(len(units)):
        own_remote(unit).start()
    token_copy(2).start()
    token_copy(3).start()
    for unit in range(len(units)):
        own_copy(unit).start()

    tempos = table_ref.shape[0]
    picked = lax.broadcasted_iota(jnp.int32, (tempos, rows), 0) == ids_ref[...]
    selector[...] = picked.astype(jnp.float32).T.astype(jnp.bfloat16)

    def make_hidden(block):
        token_copy(block).wait()
        row = near_row if block < 2 else far_row
        start = pl.multiple_of(row + (block % 2) * token_step, token_step)
        place = pl.ds(start, token_step)

        @pl.loop(0, rows // 256)
        def _(tile):
            lines = pl.ds(pl.multiple_of(tile * 256, 256), 256)
            added = jnp.dot(
                selector[lines, :], table_ref[:, place], preferred_element_type=jnp.float32
            )
            hidden[lines, place] = (hidden[lines, place].astype(jnp.float32) + added).astype(
                jnp.bfloat16
            )

    tall = rows // 2

    def near_product(unit):
        own_copy(unit).wait()
        own_remote(unit).wait_recv()
        kind, pair = units[unit]
        cols = pl.ds(pair * PAIR, PAIR)

        @pl.loop(0, 2)
        def _(tile):
            lines = pl.ds(pl.multiple_of(tile * tall, tall), tall)
            partial[kind, lines, cols] = jnp.dot(
                hidden[lines, pl.ds(near_row, near)],
                weights[kind, pl.ds(near_row, near), cols],
                preferred_element_type=jnp.float32,
            )

    def far_product(kind, first, size):
        cols = pl.ds(first, size)

        @pl.loop(0, 2)
        def _(tile):
            lines = pl.ds(pl.multiple_of(tile * tall, tall), tall)
            rounded[kind, lines, cols] = (
                partial[kind, lines, cols]
                + jnp.dot(
                    hidden[lines, pl.ds(far_row, near)],
                    weights[kind, pl.ds(far_row, near), cols],
                    preferred_element_type=jnp.float32,
                )
            ).astype(jnp.bfloat16)

    def share_beacons(kind, pair):
        slots = lax.broadcasted_iota(jnp.int32, (BEACONS, rows), 0)
        owner = lax.broadcasted_iota(jnp.int32, (BEACONS, rows), 1) // POOL
        pooling = (slots == owner).astype(jnp.bfloat16)
        pooled = jnp.dot(
            pooling,
            rounded[kind, :, pl.ds(pair * PAIR, PAIR)],
            preferred_element_type=jnp.float32,
        ) * POOL ** (-0.5)
        place = pl.ds(pl.multiple_of(rank * BEACONS, BEACONS), BEACONS)
        beacons[kind - 1, pair, place, :] = pooled.astype(jnp.bfloat16)
        for copy in beacon_copies(kind, pair):
            copy.start()

    def await_beacons(pair):
        for kind in (KEY, VALUE):
            for copy in beacon_copies(kind, pair):
                copy.wait_recv()

    slot_count = beacons.shape[2]
    factor = HEAD_DIM ** (-0.5) * math.log2(math.e)
    block_rows = 256
    contract_last = (((1,), (1,)), ((), ()))

    def attend(head):
        pair, side = head // 2, head % 2
        cols = pl.ds(head * HEAD_DIM, HEAD_DIM)
        inner = pl.ds(side * HEAD_DIM, HEAD_DIM)
        far_keys = beacons[0, pair, :, inner]
        far_values = beacons[1, pair, :, inner]
        earlier = lax.broadcasted_iota(jnp.int32, (block_rows, slot_count), 1) < rank * BEACONS
        causal = lax.broadcasted_iota(
            jnp.int32, (block_rows, block_rows), 0
        ) >= lax.broadcasted_iota(jnp.int32, (block_rows, block_rows), 1)
        for block in range(rows // block_rows):
            lines = pl.ds(block * block_rows, block_rows)
            query = rounded[QUERY, lines, cols]
            parts = [
                (
                    jnp.where(
                        earlier,
                        lax.dot_general(
                            query, far_keys, contract_last, preferred_element_type=jnp.float32
                        ),
                        LOWEST,
                    ),
                    far_values,
                ),
                (
                    jnp.where(
                        causal,
                        lax.dot_general(
                            query,
                            rounded[KEY, lines, cols],
                            contract_last,
                            preferred_element_type=jnp.float32,
                        ),
                        LOWEST,
                    ),
                    rounded[VALUE, lines, cols],
                ),
            ]
            if block:
                before = pl.ds(0, block * block_rows)
                parts.append(
                    (
                        lax.dot_general(
                            query,
                            rounded[KEY, before, cols],
                            contract_last,
                            preferred_element_type=jnp.float32,
                        ),
                        rounded[VALUE, before, cols],
                    )
                )
            highest = functools.reduce(
                jnp.maximum, [jnp.max(score, axis=1, keepdims=True) for score, _ in parts]
            )
            total = 0.0
            summed = 0.0
            for score, value in parts:
                weight = jnp.exp2((score - highest) * factor)
                total = total + jnp.sum(weight, axis=1, keepdims=True)
                summed = summed + jnp.dot(
                    weight.astype(jnp.bfloat16), value, preferred_element_type=jnp.float32
                )
            out_ref[lines, cols] = (summed / total).astype(jnp.bfloat16)

    def far_unit(unit):
        kind, pair = units[unit]
        far_product(kind, pair * PAIR, PAIR)
        if kind != QUERY:
            share_beacons(kind, pair)

    def far_chunk(index):
        kind, block = chunks[index]
        far_product(kind, block * CHUNK, CHUNK)

    work = {step: [] for step in range(count + 2)}
    work[0] += [functools.partial(make_hidden, 2), functools.partial(make_hidden, 3)]
    near_at = [1, 1, 2, 2, 4, 4]
    for unit in range(len(units)):
        work[near_at[min(unit, 5)]].append(functools.partial(near_product, unit))
    for unit in range(len(units) - 1):
        work[2 * unit + 3].append(functools.partial(far_unit, unit))
    for pair in range(pairs - 1):
        ready = 6 * pair + 8
        work[ready - 1].append(functools.partial(await_beacons, pair))
        work[ready].append(functools.partial(attend, 2 * pair))
        work[ready + 2].append(functools.partial(attend, 2 * pair + 1))
    work[count].append(functools.partial(far_chunk, count - 2))
    work[count].append(functools.partial(await_beacons, pairs - 1))
    work[count].append(functools.partial(attend, 2 * pairs - 2))
    work[count + 1].append(functools.partial(far_chunk, count - 1))
    work[count + 1].append(functools.partial(attend, 2 * pairs - 1))

    make_hidden(0)
    make_hidden(1)
    for step in range(count + 2):
        if step < count:
            x_copy(step).wait_recv()
            y_copy(step).start()
            cx_copy(step).start()
            if step + AHEAD < count:
                x_copy(step).wait_send()
                x_copy(step + AHEAD).start()
        if 1 <= step <= count:
            y_copy(step - 1).wait_recv()
            cy_copy(step - 1).start()
            cx_copy(step - 1).wait_recv()
        if step >= 2:
            cy_copy(step - 2).wait_recv()
        for task in work[step]:
            task()

    for index in range(count):
        if index + AHEAD >= count:
            x_copy(index).wait_send()
        y_copy(index).wait_send()
        cx_copy(index).wait_send()
        cy_copy(index).wait_send()
    for unit in range(len(units)):
        own_remote(unit).wait_send()
    for pair in range(pairs):
        for kind in (KEY, VALUE):
            for copy in beacon_copies(kind, pair):
                copy.wait_send()


def on_device_fused(tokens_in, tempo_ids, tempo_table, w_query, w_key, w_value):
    rows, depth = tokens_in.shape
    width = w_query.shape[1]
    pairs = width // PAIR
    units = 3 * pairs
    chunks = 2 * units
    slots = lax.axis_size("ctx") * BEACONS
    dma = pltpu.SemaphoreType.DMA
    anywhere = pl.BlockSpec(memory_space=pl.ANY)
    vmem = pl.BlockSpec(memory_space=pltpu.VMEM)
    return pl.pallas_call(
        song_kernel,
        out_shape=jax.ShapeDtypeStruct((rows, width), jnp.bfloat16),
        in_specs=[anywhere, vmem, vmem, anywhere, anywhere, anywhere],
        out_specs=vmem,
        scratch_shapes=[
            pltpu.VMEM((rows, depth), jnp.bfloat16),
            pltpu.VMEM((3, depth, width), jnp.bfloat16),
            pltpu.VMEM((3, rows, width), jnp.float32),
            pltpu.VMEM((3, rows, width), jnp.bfloat16),
            pltpu.VMEM((rows, tempo_table.shape[0]), jnp.bfloat16),
            pltpu.VMEM((2, pairs, slots, PAIR), jnp.bfloat16),
            dma((4,)),
            dma((units,)),
            dma((chunks,)),
            dma((chunks,)),
            dma((chunks,)),
            dma((chunks,)),
            dma((units,)),
            dma((units,)),
            dma((chunks,)),
            dma((chunks,)),
            dma((chunks,)),
            dma((chunks,)),
            dma((2, pairs, 3)),
            dma((2, pairs, 3)),
        ],
        compiler_params=pltpu.CompilerParams(
            collective_id=0, has_side_effects=True, vmem_limit_bytes=56 * 2**20
        ),
        cost_estimate=pl.CostEstimate(
            flops=2 * rows * depth * width * 3,
            bytes_accessed=2 * (rows * depth + 3 * depth * width),
            transcendentals=rows * rows * (width // HEAD_DIM),
        ),
    )(tokens_in, tempo_ids.reshape(1, rows), tempo_table, w_query, w_key, w_value)


def solution(mesh):
    sizes = dict(mesh.shape)

    def choose(tokens_in, tempo_ids, tempo_table, w_query, w_key, w_value):
        fused = (
            sizes["groups"] == 2
            and sizes["ctx"] == 4
            and tokens_in.shape[0] == SPAN
            and w_query.shape[0] * 4 == tokens_in.shape[1]
            and w_query.shape[1] % PAIR == 0
        )
        body = on_device_fused if fused else on_device
        return body(tokens_in, tempo_ids, tempo_table, w_query, w_key, w_value)

    in_specs = (
        P(("groups", "ctx"), None),
        P(("groups", "ctx")),
        P(),
        P("ctx", "head"),
        P("ctx", "head"),
        P("ctx", "head"),
    )
    out_specs = P(("groups", "ctx"), "head")
    return jax.shard_map(
        choose, mesh=mesh, in_specs=in_specs, out_specs=out_specs, check_vma=False
    )
```

```python
import functools
import math

import jax
import jax.numpy as jnp
from jax import lax
from jax.experimental import pallas as pl
from jax.experimental.pallas import tpu as pltpu
from jax.sharding import PartitionSpec as P

HEAD_DIM = 128
SPAN = 1024
BEACONS = 32
POOL = 32


LOWEST = -1e30


def by_heads(matrix, heads_local):
    return matrix.reshape(matrix.shape[0], heads_local, -1).transpose(1, 0, 2)


def partial_attend(queries, keys, values, allowed):
    scores = jnp.einsum(
        "hqd,hkd->hqk", queries, keys, preferred_element_type=jnp.float32
    ) * queries.shape[-1] ** (-0.5)
    masked = jnp.where(allowed, scores, LOWEST)
    highest = jnp.max(masked, axis=2)
    weights = jnp.where(allowed, jnp.exp(masked - highest[..., None]), 0.0)
    totals = jnp.sum(weights, axis=2)
    summed = jnp.einsum(
        "hqk,hkd->hqd", weights.astype(jnp.bfloat16), values, preferred_element_type=jnp.float32
    )
    return (highest, totals, summed)


def combine_partials(first, second):
    highest = jnp.maximum(first[0], second[0])
    left_factor = jnp.exp(first[0] - highest)
    right_factor = jnp.exp(second[0] - highest)
    totals = first[1] * left_factor + second[1] * right_factor
    summed = first[2] * left_factor[..., None] + second[2] * right_factor[..., None]
    return (highest, totals, summed)


def beacon_partial(
    queries, query_span, beacon_keys, beacon_values, low_rank, high_rank, group, slots_dev
):
    heads_local, query_count, head_size = queries.shape
    block_width = group * slots_dev
    start_state = (
        jnp.full((heads_local, query_count), LOWEST, jnp.float32),
        jnp.zeros((heads_local, query_count), jnp.float32),
        jnp.zeros((heads_local, query_count, head_size), jnp.float32),
    )

    def visit(block, state):
        first_slot = block * block_width
        block_keys = lax.dynamic_slice_in_dim(beacon_keys, first_slot, block_width, 1)
        block_values = lax.dynamic_slice_in_dim(beacon_values, first_slot, block_width, 1)
        slot_index = first_slot + jnp.arange(block_width, dtype=jnp.int32)
        owner = slot_index // slots_dev
        in_range = (owner >= low_rank) & (owner < high_rank)
        earlier = (slot_index // BEACONS)[None, :] < query_span[:, None]
        allowed = (in_range[None, :] & earlier)[None]
        return combine_partials(state, partial_attend(queries, block_keys, block_values, allowed))

    first_block = low_rank // group
    last_block = (high_rank + group - 1) // group
    return lax.fori_loop(first_block, last_block, visit, start_state)


def on_device(tokens_in, tempo_ids, tempo_table, w_query, w_key, w_value):
    row_count = tokens_in.shape[0]
    col_width = w_query.shape[1]
    heads_local = col_width // HEAD_DIM
    ctx_count = lax.axis_size("ctx")
    ctx_rank = lax.axis_index("ctx")
    spans_dev = row_count // SPAN
    slots_dev = spans_dev * BEACONS
    target = max(1, 256 // slots_dev)
    group = min(ctx_count, 1 << target.bit_length() - 1)
    selector = (
        tempo_ids[:, None] == jnp.arange(tempo_table.shape[0], dtype=jnp.int32)[None, :]
    ).astype(jnp.bfloat16)
    hidden = (
        tokens_in.astype(jnp.float32)
        + jnp.dot(selector, tempo_table, preferred_element_type=jnp.float32)
    ).astype(jnp.bfloat16)
    pieces = (
        lax.all_gather(w_query, "ctx", axis=0, tiled=True),
        lax.all_gather(w_key, "ctx", axis=0, tiled=True),
        lax.all_gather(w_value, "ctx", axis=0, tiled=True),
    )
    projected = tuple(
        (jnp.dot(hidden, piece, preferred_element_type=jnp.float32) for piece in pieces)
    )
    queries = projected[0].astype(jnp.bfloat16)
    keys = projected[1].astype(jnp.bfloat16)
    values = projected[2].astype(jnp.bfloat16)
    pool_scale = POOL ** (-0.5)
    own_keys = (
        jnp.sum(keys.reshape(slots_dev, POOL, col_width).astype(jnp.float32), axis=1) * pool_scale
    ).astype(jnp.bfloat16)
    own_values = (
        jnp.sum(values.reshape(slots_dev, POOL, col_width).astype(jnp.float32), axis=1) * pool_scale
    ).astype(jnp.bfloat16)
    every_keys, every_values = (
        lax.all_gather(own_keys, "ctx", axis=0, tiled=True),
        lax.all_gather(own_values, "ctx", axis=0, tiled=True),
    )
    beacon_keys = by_heads(every_keys, heads_local)
    beacon_values = by_heads(every_values, heads_local)
    query_heads = by_heads(queries, heads_local)
    local_span = jnp.arange(row_count, dtype=jnp.int32) // SPAN
    own_span = ctx_rank * spans_dev + local_span

    def fold_spans(matrix):
        return by_heads(matrix, heads_local)

    causal = (
        jnp.arange(SPAN, dtype=jnp.int32)[:, None] >= jnp.arange(SPAN, dtype=jnp.int32)[None, :]
    )[None]
    inside = partial_attend(fold_spans(queries), fold_spans(keys), fold_spans(values), causal)
    inside = (inside[0], inside[1], inside[2])
    upper_rank = ctx_rank + 1
    remote = beacon_partial(
        query_heads,
        own_span,
        beacon_keys,
        beacon_values,
        jnp.zeros((), jnp.int32),
        upper_rank,
        group,
        slots_dev,
    )
    highest, totals, summed = combine_partials(inside, remote)
    attended = summed / totals[..., None]
    return attended.transpose(1, 0, 2).reshape(row_count, col_width).astype(jnp.bfloat16)


CHUNK = HEAD_DIM
PAIR = 2 * HEAD_DIM
AHEAD = 3
MESH = pl.DeviceIdType.MESH
QUERY, KEY, VALUE = 0, 1, 2


def song_kernel(
    tokens_hbm,
    ids_hbm,
    table_hbm,
    wq_hbm,
    wk_hbm,
    wv_hbm,
    out_ref,
    hidden,
    weights,
    partial,
    rounded,
    selector,
    beacons,
    ids_ref,
    table_ref,
    small_sem,
    token_sem,
    own_sem,
    x_send,
    x_recv,
    y_send,
    y_recv,
    own_send,
    own_recv,
    cx_send,
    cx_recv,
    cy_send,
    cy_recv,
    b_send,
    b_recv,
):
    rows, depth = hidden.shape
    shard, width = wq_hbm.shape
    pairs = width // PAIR
    half = shard // 2
    near = 2 * shard
    sources = (wq_hbm, wk_hbm, wv_hbm)

    song = lax.axis_index("groups")
    rank = lax.axis_index("ctx")
    chip, core = rank // 2, rank % 2
    far_chip = 1 - chip
    sibling = {"ctx": chip * 2 + 1 - core}
    across = {"ctx": far_chip * 2 + core}
    diagonal = {"ctx": far_chip * 2 + 1 - core}
    twin = {"groups": 1 - song}

    near_row = pl.multiple_of(chip * near, near)
    far_row = pl.multiple_of(far_chip * near, near)
    units = 3 * pairs
    count = 2 * units

    def unit_of(unit):
        return (unit + 1) % 3, unit // 3

    def chunk_of(index):
        kind, pair = unit_of(index // 2)
        return kind, pair * 2 + index % 2

    def columns(block, size):
        return pl.ds(pl.multiple_of(block * size, size), size)

    def spot(index, owner_chip, owner_core, part):
        kind, block = chunk_of(index)
        row = pl.multiple_of((owner_chip * 2 + owner_core) * shard + part * half, half)
        return weights.at[kind, pl.ds(row, half), columns(block, CHUNK)]

    def x_copy(index, source):
        block = chunk_of(index)[1]
        begin = pl.multiple_of(song * half, half)
        return pltpu.make_async_remote_copy(
            src_ref=source.at[pl.ds(begin, half), columns(block, CHUNK)],
            dst_ref=spot(index, chip, core, song),
            send_sem=x_send.at[index],
            recv_sem=x_recv.at[index],
            device_id=across,
            device_id_type=MESH,
        )

    def x_start(index):
        for kind, source in enumerate(sources):

            @pl.when(chunk_of(index)[0] == kind)
            def _():
                x_copy(index, source).start()

    def y_copy(index):
        place = spot(index, far_chip, core, song)
        return pltpu.make_async_remote_copy(
            src_ref=place,
            dst_ref=place,
            send_sem=y_send.at[index],
            recv_sem=y_recv.at[index],
            device_id=twin,
            device_id_type=MESH,
        )

    def core_copy(index, part, send, recv):
        place = spot(index, far_chip, core, part)
        return pltpu.make_async_remote_copy(
            src_ref=place,
            dst_ref=place,
            send_sem=send.at[index],
            recv_sem=recv.at[index],
            device_id=sibling,
            device_id_type=MESH,
        )

    def cx_copy(index):
        return core_copy(index, song, cx_send, cx_recv)

    def cy_copy(index):
        return core_copy(index, 1 - song, cy_send, cy_recv)

    def own_place(unit):
        kind, pair = unit_of(unit)
        row = pl.multiple_of(rank * shard, shard)
        return weights.at[kind, pl.ds(row, shard), columns(pair, PAIR)]

    def own_source(unit):
        if not isinstance(unit, int):
            return own_place(unit)
        kind, pair = unit_of(unit)
        return sources[kind].at[:, columns(pair, PAIR)]

    def own_copy(unit):
        return pltpu.make_async_copy(own_source(unit), own_place(unit), own_sem.at[unit])

    def own_remote(unit):
        return pltpu.make_async_remote_copy(
            src_ref=own_source(unit),
            dst_ref=own_place(unit),
            send_sem=own_send.at[unit],
            recv_sem=own_recv.at[unit],
            device_id=sibling,
            device_id_type=MESH,
        )

    token_step = depth // 4

    def token_place(block):
        side = (chip + block // 2) % 2
        start = pl.multiple_of(side * near + (block % 2) * token_step, token_step)
        return pl.ds(start, token_step)

    def token_copy(block):
        place = token_place(block)
        return pltpu.make_async_copy(
            tokens_hbm.at[:, place], hidden.at[:, place], token_sem.at[block]
        )

    def beacon_copies(kind, pair):
        place = beacons.at[kind - 1, pair, pl.ds(pl.multiple_of(rank * BEACONS, BEACONS), BEACONS)]
        result = []
        for number, target in enumerate((sibling, across, diagonal)):
            result.append(
                pltpu.make_async_remote_copy(
                    src_ref=place,
                    dst_ref=place,
                    send_sem=b_send.at[kind - 1, pair, number],
                    recv_sem=b_recv.at[kind - 1, pair, number],
                    device_id=target,
                    device_id_type=MESH,
                )
            )
        return result

    ids_copy = pltpu.make_async_copy(ids_hbm, ids_ref, small_sem.at[0])
    table_copy = pltpu.make_async_copy(table_hbm, table_ref, small_sem.at[1])
    ids_copy.start()
    table_copy.start()
    token_copy(0).start()
    token_copy(1).start()
    barrier = pltpu.get_barrier_semaphore()
    partners = (sibling, across, diagonal, twin)
    for target in partners:
        pl.semaphore_signal(barrier, inc=1, device_id=target, device_id_type=MESH)
    pl.semaphore_wait(barrier, len(partners))

    for index in range(AHEAD):
        x_copy(index, sources[chunk_of(index)[0]]).start()
    for unit in range(units):
        own_remote(unit).start()
    token_copy(2).start()
    token_copy(3).start()
    for unit in range(units):
        own_copy(unit).start()

    tempos = table_ref.shape[0]
    ids_copy.wait()
    table_copy.wait()
    picked = lax.broadcasted_iota(jnp.int32, (tempos, rows), 0) == ids_ref[...]
    selector[...] = picked.astype(jnp.float32).T.astype(jnp.bfloat16)

    def make_hidden(block):
        token_copy(block).wait()
        place = token_place(block)

        @pl.loop(0, rows // 256)
        def _(tile):
            lines = pl.ds(pl.multiple_of(tile * 256, 256), 256)
            added = jnp.dot(
                selector[lines, :], table_ref[:, place], preferred_element_type=jnp.float32
            )
            hidden[lines, place] = (hidden[lines, place].astype(jnp.float32) + added).astype(
                jnp.bfloat16
            )

    tall = rows // 2

    def near_product(unit):
        own_copy(unit).wait()
        own_remote(unit).wait_recv()
        kind, pair = unit_of(unit)
        cols = columns(pair, PAIR)

        @pl.loop(0, 2)
        def _(tile):
            lines = columns(tile, tall)
            partial[kind, lines, cols] = jnp.dot(
                hidden[lines, pl.ds(near_row, near)],
                weights[kind, pl.ds(near_row, near), cols],
                preferred_element_type=jnp.float32,
            )

    def far_product(kind, cols, tile):
        lines = columns(tile, tall)
        rounded[kind, lines, cols] = (
            partial[kind, lines, cols]
            + jnp.dot(
                hidden[lines, pl.ds(far_row, near)],
                weights[kind, pl.ds(far_row, near), cols],
                preferred_element_type=jnp.float32,
            )
        ).astype(jnp.bfloat16)

    def share_beacons(kind, pair):
        slots = lax.broadcasted_iota(jnp.int32, (BEACONS, rows), 0)
        owner = lax.broadcasted_iota(jnp.int32, (BEACONS, rows), 1) // POOL
        pooling = (slots == owner).astype(jnp.bfloat16)
        pooled = jnp.dot(
            pooling,
            rounded[kind, :, columns(pair, PAIR)],
            preferred_element_type=jnp.float32,
        ) * POOL ** (-0.5)
        place = pl.ds(pl.multiple_of(rank * BEACONS, BEACONS), BEACONS)
        beacons[kind - 1, pair, place, :] = pooled.astype(jnp.bfloat16)
        for copy in beacon_copies(kind, pair):
            copy.start()

    def await_beacons(pair):
        for kind in (KEY, VALUE):
            for copy in beacon_copies(kind, pair):
                copy.wait_recv()

    slot_count = beacons.shape[2]
    factor = HEAD_DIM ** (-0.5) * math.log2(math.e)
    block_rows = 256
    contract_last = (((1,), (1,)), ((), ()))

    def attend(head):
        pair, side = head // 2, head % 2
        cols = columns(head, HEAD_DIM)
        inner = columns(side, HEAD_DIM)
        far_keys = beacons[0, pair, :, inner]
        far_values = beacons[1, pair, :, inner]
        earlier = lax.broadcasted_iota(jnp.int32, (block_rows, slot_count), 1) < rank * BEACONS
        causal = lax.broadcasted_iota(
            jnp.int32, (block_rows, block_rows), 0
        ) >= lax.broadcasted_iota(jnp.int32, (block_rows, block_rows), 1)
        for block in range(rows // block_rows):
            lines = pl.ds(block * block_rows, block_rows)
            query = rounded[QUERY, lines, cols]
            parts = [
                (
                    jnp.where(
                        earlier,
                        lax.dot_general(
                            query, far_keys, contract_last, preferred_element_type=jnp.float32
                        ),
                        LOWEST,
                    ),
                    far_values,
                ),
                (
                    jnp.where(
                        causal,
                        lax.dot_general(
                            query,
                            rounded[KEY, lines, cols],
                            contract_last,
                            preferred_element_type=jnp.float32,
                        ),
                        LOWEST,
                    ),
                    rounded[VALUE, lines, cols],
                ),
            ]
            if block:
                before = pl.ds(0, block * block_rows)
                parts.append(
                    (
                        lax.dot_general(
                            query,
                            rounded[KEY, before, cols],
                            contract_last,
                            preferred_element_type=jnp.float32,
                        ),
                        rounded[VALUE, before, cols],
                    )
                )
            highest = functools.reduce(
                jnp.maximum, [jnp.max(score, axis=1, keepdims=True) for score, _ in parts]
            )
            total = 0.0
            summed = 0.0
            for score, value in parts:
                weight = jnp.exp2((score - highest) * factor)
                total = total + jnp.sum(weight, axis=1, keepdims=True)
                summed = summed + jnp.dot(
                    weight.astype(jnp.bfloat16), value, preferred_element_type=jnp.float32
                )
            out_ref[lines, cols] = (summed / total).astype(jnp.bfloat16)

    last = units - 1

    @pl.loop(0, 4)
    def _(block):
        make_hidden(block)

    def forward_y(index):
        y_copy(index).wait_recv()
        cy_copy(index).start()
        cx_copy(index).wait_recv()

    @pl.loop(0, count + 2)
    def _(step):
        @pl.when(step < count)
        def _():
            x_copy(step, wq_hbm).wait_recv()
            y_copy(step).start()
            cx_copy(step).start()

        @pl.when(step + AHEAD < count)
        def _():
            x_copy(step, wq_hbm).wait_send()
            x_start(step + AHEAD)

        @pl.when((step >= 1) & (step < count))
        def _():
            forward_y(step - 1)

        @pl.when(step == count + 1)
        def _():
            forward_y(step - 2)

        @pl.when(step >= 2)
        def _():
            cy_copy(step - 2).wait_recv()

        @pl.when(step < units)
        def _():
            near_product(step)

        unit = (step - 3) // 2

        @pl.when((step >= 3) & ((unit < last - 1) | (step == 2 * last + 1)))
        def _():
            kind, pair = unit_of(unit)
            tile = (step - 3) % 2
            far_product(kind, columns(pair, PAIR), tile)

            @pl.when(unit == last - 1)
            def _():
                far_product(kind, columns(pair, PAIR), 1)

            @pl.when((kind != QUERY) & ((tile == 1) | (unit == last - 1)))
            def _():
                share_beacons(kind, pair)

        @pl.when(step >= count)
        def _():
            kind, block = chunk_of(step - 2)

            @pl.loop(0, 2)
            def _(tile):
                far_product(kind, columns(block, CHUNK), tile)

        phase = (step - 8) % 6
        final = step >= count
        ready = (step >= 8) & ((phase == 0) | (phase == 2)) & (step < count - 1)

        @pl.when((ready & (phase == 0)) | (step == count))
        def _():
            await_beacons(jnp.where(final, pairs - 1, (step - 8) // 6))

        @pl.when(ready | final)
        def _():
            attend(
                jnp.where(
                    final, 2 * pairs - 2 + step - count, (step - 8) // 6 * 2 + phase // 2
                )
            )

    for index in range(count):
        if index + AHEAD >= count:
            x_copy(index, sources[chunk_of(index)[0]]).wait_send()
        y_copy(index).wait_send()
        cx_copy(index).wait_send()
        cy_copy(index).wait_send()
    for unit in range(units):
        own_remote(unit).wait_send()
    for pair in range(pairs):
        for kind in (KEY, VALUE):
            for copy in beacon_copies(kind, pair):
                copy.wait_send()


def on_device_fused(tokens_in, tempo_ids, tempo_table, w_query, w_key, w_value):
    rows, depth = tokens_in.shape
    width = w_query.shape[1]
    pairs = width // PAIR
    units = 3 * pairs
    chunks = 2 * units
    slots = lax.axis_size("ctx") * BEACONS
    dma = pltpu.SemaphoreType.DMA
    anywhere = pl.BlockSpec(memory_space=pl.ANY)
    vmem = pl.BlockSpec(memory_space=pltpu.VMEM)
    return pl.pallas_call(
        song_kernel,
        out_shape=pltpu.VMEM((rows, width), jnp.bfloat16),
        in_specs=[anywhere] * 6,
        out_specs=vmem,
        scratch_shapes=[
            pltpu.VMEM((rows, depth), jnp.bfloat16),
            pltpu.VMEM((3, depth, width), jnp.bfloat16),
            pltpu.VMEM((3, rows, width), jnp.float32),
            pltpu.VMEM((3, rows, width), jnp.bfloat16),
            pltpu.VMEM((rows, tempo_table.shape[0]), jnp.bfloat16),
            pltpu.VMEM((2, pairs, slots, PAIR), jnp.bfloat16),
            pltpu.VMEM((1, rows), jnp.int32),
            pltpu.VMEM(tempo_table.shape, jnp.bfloat16),
            dma((2,)),
            dma((4,)),
            dma((units,)),
            dma((chunks,)),
            dma((chunks,)),
            dma((chunks,)),
            dma((chunks,)),
            dma((units,)),
            dma((units,)),
            dma((chunks,)),
            dma((chunks,)),
            dma((chunks,)),
            dma((chunks,)),
            dma((2, pairs, 3)),
            dma((2, pairs, 3)),
        ],
        compiler_params=pltpu.CompilerParams(
            collective_id=0, has_side_effects=True, vmem_limit_bytes=56 * 2**20
        ),
        cost_estimate=pl.CostEstimate(
            flops=2 * rows * depth * width * 3,
            bytes_accessed=2 * (rows * depth + 3 * depth * width),
            transcendentals=rows * rows * (width // HEAD_DIM),
        ),
    )(tokens_in, tempo_ids.reshape(1, rows), tempo_table, w_query, w_key, w_value)


def solution(mesh):
    sizes = dict(mesh.shape)

    def choose(tokens_in, tempo_ids, tempo_table, w_query, w_key, w_value):
        fused = (
            sizes["groups"] == 2
            and sizes["ctx"] == 4
            and tokens_in.shape[0] == SPAN
            and w_query.shape[0] * 4 == tokens_in.shape[1]
            and w_query.shape[1] % PAIR == 0
        )
        body = on_device_fused if fused else on_device
        return body(tokens_in, tempo_ids, tempo_table, w_query, w_key, w_value)

    in_specs = (
        P(("groups", "ctx"), None),
        P(("groups", "ctx")),
        P(),
        P("ctx", "head"),
        P("ctx", "head"),
        P("ctx", "head"),
    )
    out_specs = P(("groups", "ctx"), "head")
    return jax.shard_map(
        choose, mesh=mesh, in_specs=in_specs, out_specs=out_specs, check_vma=False
    )
```
